32 devices in a mesh: dp: 8 (over z, x), expert: 4 (over y, core).
Axes of the slice: x: 2, y: 2, z: 4, core: 2. Of those that a mesh axis runs over, the one named last changes fastest.
Arguments:
- tokens: bfloat16 [1024, 3072], P('dp', 'expert'), may hold values from -6 to 6
- suffix_cotangent: bfloat16 [512, 3072], P('dp', 'expert'), may hold values from -6 to 6
- prefix_partials: bfloat16 [32, 32, 3072], P('dp', None, 'expert'), may hold values from -6 to 6
- prefix_of_seq: int32 [32], P('dp'), may hold values from 0 to 15
- expert_ids: int32 [1024, 2], P('dp'), may hold values from 0 to 3, all different within a row; in each aligned block of 128 rows (0 to 127, 128 to 255, ...) at most 80 rows name the same one
- router_weight: bfloat16 [3072, 4], P('expert'), may hold values from -0.109375 to 0.109375
- gate_weight: bfloat16 [4, 3072, 8192], P('expert', None, 'dp'), may hold values from -0.109375 to 0.109375
- up_weight: bfloat16 [4, 3072, 8192], P('expert', None, 'dp'), may hold values from -0.109375 to 0.109375
- down_weight: bfloat16 [4, 8192, 3072], P('expert', 'dp'), may hold values from -0.0625 to 0.0625
- gate_pre: bfloat16 [4, 640, 8192], P('expert', None, 'dp'), may hold values from -6 to 6
- up_pre: bfloat16 [4, 640, 8192], P('expert', None, 'dp'), may hold values from -6 to 6
Outputs:
- d_tokens: bfloat16 [1024, 3072], P('dp', 'expert')
- d_gate: bfloat16 [4, 3072, 8192], P('expert', None, 'dp')
- d_up: bfloat16 [4, 3072, 8192], P('expert', None, 'dp')
- d_down: bfloat16 [4, 8192, 3072], P('expert', 'dp')
The draws below stay inside these ranges and needn't reach their ends.
Inputs may be any that keep to these rules, and one draw needn't show every extreme that they name: `expert_ids`: each row names 2 different experts. Among the rows of one index of dp, each expert is named at most 80 times, a bound that some block reaches. `prefix_of_seq`: block b of the 16 prefix blocks is owned by index b // 2 of dp.
All inputs are finite; a program needn't handle non-finite values.
Results may differ from the reference program's by a relative error of at most 0.025.
Values may be sent and summed in bfloat16 or wider, within the bound.
No kernel may reach another device: no remote copies, remote signals or barrier semaphores. Data moves between devices by JAX's collectives and lax.ppermute only.
A program may use at most 128 MiB of HBM per device.

```python
import math
import jax
import jax.numpy as jnp
import numpy as np
from jax import lax

D = 3072
FF = 8192
TOP = 2
PBLK = 32
PREF_DP = 2
SUFLEN = 16
SEQ_DP = 4
EXPERTS = 4
TOK_DP = 128
CAP = 80
NPB = 16
TOKENS = 1024
N_DP = 8


def place_ends(array, rng, smallest, largest):
    spot = [jax.random.randint(jax.random.fold_in(rng, axis), (), 0, length) for axis, length in enumerate(array.shape)]
    longest = array.shape.index(max(array.shape))
    beside = spot[:longest] + [(spot[longest] + 1) % array.shape[longest]] + spot[longest + 1:]
    return array.at[tuple(spot)].set(smallest).at[tuple(beside)].set(largest)


def block_levels(key, dims, shards, low, largest):
    level, own = 1.0, jax.random.fold_in(key, 6)
    for position, parts in shards:
        heights = jnp.exp(jax.random.uniform(jax.random.fold_in(own, position), (parts,), jnp.float32, low / len(shards), largest / len(shards)))
        level = level * jnp.repeat(heights, dims[position] // parts).reshape([-1 if axis == position else 1 for axis in range(len(dims))])
    return level


def rank_bounds(amount, skew):
    portions = [(1 << 20) // math.isqrt(standing ** skew) + 1 for standing in range(1, amount + 1)]
    deviation = 1 + sum(portions) // (1 << 30)
    return np.cumsum(np.array([max(1, weight // deviation) for weight in portions]))


def ranked(rng, shape, amount, skew):
    listing = rank_bounds(amount, skew)
    lot = jax.random.randint(jax.random.fold_in(rng, 1), shape, 0, int(listing[amount - 1]))
    grade = jnp.searchsorted(jnp.asarray(listing, jnp.int32), lot, side="right")
    return jax.random.permutation(jax.random.fold_in(rng, 2), amount)[grade].astype(jnp.int32)


def shared_out(key, own, number, rows, count, top, limit, skew):
    sequence = jax.random.permutation(key, count)
    heavy_load, ordinary = shares(count, rows * top, limit, skew, True), shares(count, rows * top, limit, skew, False)
    places = jnp.arange(count)

    def named(lengths, rotation):
        used = int((lengths > 0).sum())
        fixed = max(1, used // 4)
        passed = fixed + (places - fixed + rotation * (used - fixed)) % max(1, count - fixed)
        return jnp.zeros((count,), jnp.int32).at[sequence[jnp.where(places < fixed, places, passed)]].set(jnp.asarray(lengths, jnp.int32))

    lengths = jnp.where(number % 4 == 0, named(heavy_load, number // 4), named(ordinary, number - number // 4 - 1))
    mixed = jax.random.permutation(jax.random.fold_in(own, 3), count)
    giver, receiver = mixed[0:count // 2 * 2:2], mixed[1:count // 2 * 2:2]
    slack = jnp.minimum(lengths[giver] - 1, limit - lengths[receiver]) // 2
    slack = jnp.where((giver == sequence[0]) | (receiver == sequence[0]) | (lengths[receiver] == 0), 0, jnp.maximum(slack, 0))
    passed = jax.random.randint(jax.random.fold_in(own, 4), (count // 2,), 0, 1 << 20) % (slack + 1)
    lengths = lengths.at[giver].add(-passed).at[receiver].add(passed)
    items = jnp.searchsorted(jnp.cumsum(lengths), jnp.arange(rows * top), side="right").astype(jnp.int32)
    table = items.reshape(top, rows).T
    table = table[jax.random.permutation(jax.random.fold_in(own, 1), rows)]
    rotation = jax.random.randint(jax.random.fold_in(own, 2), (rows, 1), 0, top)
    return jnp.take_along_axis(table, (jnp.arange(top)[None, :] + rotation) % top, axis=1)


def shares(count, total, limit, skew, full):
    weights = [(1 << 20) // math.isqrt(rank ** skew) + 1 for rank in range(1, count + 1)]
    largest = limit if full else min(limit, max(-(-total // count), total * weights[0] // sum(weights)))
    least = 1 if total - largest >= count - 1 else 0
    holding, spare = [largest] + [least] * (count - 1), total - largest - least * (count - 1)
    while spare > 0:
        candidates = [i for i in range(1, count) if holding[i] < largest] or [i for i in range(1, count) if holding[i] < limit]
        pool, remaining = sum([weights[i] for i in candidates]), spare
        for i in candidates:
            more = min(limit - holding[i], max(1, remaining * weights[i] // pool), spare)
            holding[i] = holding[i] + more
            spare = spare - more
    return np.array(holding)


def noise(rng, dims, spread, reach, cuts=(), kind=jnp.bfloat16):
    level = block_levels(rng, dims, cuts, -0.22, 0.18) if cuts else 1.0
    array = jax.random.normal(rng, dims, jnp.float32) * spread * level
    return jnp.minimum(jnp.maximum(array, -reach), reach).astype(kind)


def setup_inputs(seed: int = 0) -> dict:
    key_list = jax.random.split(jax.random.key(seed), 12)
    tokens = noise(key_list[0], (TOKENS, D), 1.0, 6.0, ((0, 8), (1, 4)))
    suffix_cotangent = noise(key_list[1], (N_DP * SEQ_DP * SUFLEN, D), 1.0, 6.0, ((0, 8), (1, 4)))
    prefix_partials = noise(key_list[2], (N_DP * SEQ_DP, PBLK, D), 1.0, 6.0, ((0, 8), (2, 4)))
    prefix_of_seq = place_ends(ranked(key_list[3], (N_DP * SEQ_DP,), NPB, 2), jax.random.fold_in(key_list[3], 3), 0, NPB - 1).astype(jnp.int32)
    expert_ids_keys = jax.random.split(jax.random.fold_in(key_list[4], 1), TOKENS // TOK_DP)
    expert_ids_turns = jax.random.permutation(jax.random.fold_in(key_list[4], 3), TOKENS // TOK_DP)
    expert_ids = jax.vmap(lambda own, number: shared_out(jax.random.fold_in(key_list[4], 2), own, number, TOK_DP, EXPERTS, TOP, CAP, 1))(expert_ids_keys, expert_ids_turns).reshape((TOKENS, TOP))
    router_weight = noise(key_list[5], (D, EXPERTS), D ** -0.5, 0.109375, ((0, 4),))
    gate_weight = noise(key_list[6], (EXPERTS, D, FF), D ** -0.5, 0.109375, ((0, 4), (2, 8)))
    up_weight = noise(key_list[7], (EXPERTS, D, FF), D ** -0.5, 0.109375, ((0, 4), (2, 8)))
    down_weight = noise(key_list[8], (EXPERTS, FF, D), FF ** -0.5, 0.0625, ((0, 4), (1, 8)))
    gate_pre = noise(key_list[9], (EXPERTS, N_DP * CAP, FF), 1.0, 6.0, ((0, 4), (2, 8)))
    up_pre = noise(key_list[10], (EXPERTS, N_DP * CAP, FF), 1.0, 6.0, ((0, 4), (2, 8)))
    return {"tokens": tokens, "suffix_cotangent": suffix_cotangent, "prefix_partials": prefix_partials, "prefix_of_seq": prefix_of_seq, "expert_ids": expert_ids, "router_weight": router_weight, "gate_weight": gate_weight, "up_weight": up_weight, "down_weight": down_weight, "gate_pre": gate_pre, "up_pre": up_pre}


def silu_parts(values):
    sigmoid_v = jax.nn.sigmoid(values)
    return values * sigmoid_v, sigmoid_v * (1.0 + values * (1.0 - sigmoid_v))


def one_expert(inputs):
    rows_x, rows_g, slot_weight, gate_w, up_w, down_w, gate_saved, up_saved = inputs
    gate_act = gate_saved.astype(jnp.float32)
    up_act = up_saved.astype(jnp.float32)
    activation, slope = silu_parts(gate_act)
    hidden = activation * up_act
    d_hidden = jnp.dot(rows_g, down_w.T, preferred_element_type=jnp.float32)
    dots = jnp.sum(hidden * d_hidden, axis=1)
    weight_col = slot_weight.astype(jnp.float32)[:, None]
    scaled = weight_col * d_hidden
    weighted = (weight_col * hidden).astype(jnp.bfloat16)
    d_gate_act = (scaled * up_act * slope).astype(jnp.bfloat16)
    d_up_act = (scaled * activation).astype(jnp.bfloat16)
    grad_down = jnp.dot(weighted.T, rows_g, preferred_element_type=jnp.float32).astype(jnp.bfloat16)
    grad_gate = jnp.dot(rows_x.T, d_gate_act, preferred_element_type=jnp.float32).astype(jnp.bfloat16)
    grad_up = jnp.dot(rows_x.T, d_up_act, preferred_element_type=jnp.float32).astype(jnp.bfloat16)
    shard_width = FF // N_DP

    def add_shard(total, shard):
        lower = (shard * shard_width).astype(jnp.int32)
        part_gate = lax.dynamic_slice_in_dim(d_gate_act, lower, shard_width, 1)
        part_up = lax.dynamic_slice_in_dim(d_up_act, lower, shard_width, 1)
        gate_part = lax.dynamic_slice_in_dim(gate_w, lower, shard_width, 1)
        up_part = lax.dynamic_slice_in_dim(up_w, lower, shard_width, 1)
        term = jnp.dot(part_gate, gate_part.T, preferred_element_type=jnp.float32)
        term = term + jnp.dot(part_up, up_part.T, preferred_element_type=jnp.float32)
        rounded = lax.optimization_barrier(term.astype(jnp.bfloat16))
        return total + rounded.astype(jnp.float32), None

    start_total = jnp.zeros((rows_x.shape[0], D), jnp.float32)
    dx_rows, _ = lax.scan(add_shard, start_total, jnp.arange(N_DP, dtype=jnp.int32))
    return grad_gate, grad_up, grad_down, dx_rows, dots


def reference(tokens, suffix_cotangent, prefix_partials, prefix_of_seq, expert_ids, router_weight, gate_weight, up_weight, down_weight, gate_pre, up_pre):
    owners = (prefix_of_seq[:, None] == jnp.arange(NPB, dtype=jnp.int32)[None, :]).astype(jnp.float32)
    flat_partials = prefix_partials.reshape(N_DP * SEQ_DP, PBLK * D).astype(jnp.float32)
    prefix_sum = jnp.dot(owners.T, flat_partials, precision=lax.Precision.HIGHEST)
    prefix_cot = prefix_sum.astype(jnp.bfloat16).reshape(N_DP, PREF_DP * PBLK, D)
    suffix_rows = suffix_cotangent.reshape(N_DP, SEQ_DP * SUFLEN, D)
    cot = jnp.concatenate([prefix_cot, suffix_rows], axis=1).reshape(TOKENS, D)

    logits = jnp.dot(tokens, router_weight, preferred_element_type=jnp.float32)
    chosen = (expert_ids[:, :, None] == jnp.arange(EXPERTS, dtype=jnp.int32)[None, None, :]).astype(jnp.float32)
    picked = jnp.sum(logits[:, None, :] * chosen, axis=2)
    first_prob = jax.nn.sigmoid(picked[:, 0] - picked[:, 1])
    second_prob = 1.0 - first_prob
    probs = jnp.stack([first_prob, second_prob], axis=1)

    block_ids = expert_ids.reshape(N_DP, TOK_DP * TOP)
    member = (block_ids[:, :, None] == jnp.arange(EXPERTS, dtype=jnp.int32)[None, None, :]).astype(jnp.int32)
    before = jnp.cumsum(member, axis=1) - member
    slot_index = jnp.sum(before * member, axis=2)
    source = jnp.arange(N_DP, dtype=jnp.int32)[:, None]
    dest = (source * CAP + slot_index).reshape(-1).astype(jnp.int32)
    expert_flat = block_ids.reshape(-1).astype(jnp.int32)
    row_total = N_DP * CAP
    rows_x = jnp.zeros((EXPERTS, row_total, D), tokens.dtype).at[expert_flat, dest].set(jnp.repeat(tokens, TOP, axis=0))
    rows_g = jnp.zeros((EXPERTS, row_total, D), cot.dtype).at[expert_flat, dest].set(jnp.repeat(cot, TOP, axis=0))
    slot_weight = jnp.zeros((EXPERTS, row_total), jnp.bfloat16).at[expert_flat, dest].set(probs.reshape(-1).astype(jnp.bfloat16))

    grad_gate, grad_up, grad_down, dx_all, dots_all = lax.map(one_expert, (rows_x, rows_g, slot_weight, gate_weight, up_weight, down_weight, gate_pre, up_pre))
    dx_pair = dx_all[expert_flat, dest].reshape(TOKENS, TOP, D)
    dots_pair = dots_all[expert_flat, dest].reshape(TOKENS, TOP)
    d_logit = first_prob * second_prob * (dots_pair[:, 0] - dots_pair[:, 1])
    d_logits = d_logit[:, None] * (chosen[:, 0, :] - chosen[:, 1, :])
    dx_router = jnp.dot(d_logits, router_weight.astype(jnp.float32).T, precision=lax.Precision.HIGHEST)
    d_tokens = (dx_pair[:, 0] + dx_pair[:, 1] + dx_router).astype(jnp.bfloat16)
    return d_tokens, grad_gate, grad_up, grad_down
```

```python
import functools

import jax
import jax.numpy as jnp
from jax import lax
from jax.experimental import pallas as pl
from jax.experimental.pallas import tpu as pltpu
from jax.sharding import PartitionSpec as P

PREF_DP = 2
AXES = ("dp", "expert")
F32, BF16 = jnp.float32, jnp.bfloat16
MIB = 1 << 20
GFLOP = 10**9
X, Z1, Z2, Y, C = (1, 0), (2, 0), (4, 0), (0, 2), (0, 1)


def xor(a, b):
    return a[0] ^ b[0], a[1] ^ b[1]


def send(value, mask):
    dps, experts = lax.axis_size("dp"), lax.axis_size("expert")
    pairs = [
        (d * experts + e, (d ^ mask[0]) * experts + (e ^ mask[1]))
        for d in range(dps)
        for e in range(experts)
    ]
    return lax.ppermute(value, AXES, pairs)


def bits(count, start):
    return [1 << b for b in range(start, count.bit_length() - 1)]


TREE = [
    (Z2, (0, 0)),
    (X, (0, 0)),
    (Y, (0, 0)),
    (Z1, (0, 0)),
    (Y, (1, 0)),
    (Z1, (0, 2)),
    (X, (4, 0)),
    (Y, (4, 0)),
    (Z1, (4, 0)),
    (X, (2, 0)),
    (Y, (5, 0)),
    (Z1, (4, 2)),
    (X, (6, 0)),
    (Y, (3, 0)),
    (Z1, (5, 2)),
]
X_AT = (5, 0)
SMALL_AT = ((2, 0), (4, 0), (6, 0), (6, 2))


def whole_extra(rows):
    base = rows[None, None]
    for bit in bits(lax.axis_size("dp"), 3):
        base = jnp.concatenate([base, send(base, (bit, 0))], axis=1)
    for bit in bits(lax.axis_size("expert"), 2):
        base = jnp.concatenate([base, send(base, (0, bit))], axis=0)
    return base


def gather_tree(rows):
    pieces = {(0, 0): whole_extra(rows)}
    for link, mask in TREE:
        pieces[xor(link, mask)] = send(pieces[mask], link)
    return pieces


def gather_column(rows, token):
    base, _ = lax.optimization_barrier((whole_extra(rows), token))
    two, one = send(base, Z2), send(base, Z1)
    return jnp.stack([base, one, two, send(two, Z1)])


class SmallGather:
    def __init__(self, logits, router_t, rest):
        self.logits, self.routers, self.rest, self.whole = logits, router_t, rest, None
        self.todo = [(0, bit) for bit in bits(lax.axis_size("expert"), 0)]
        self.todo += [(bit, 0) for bit in bits(lax.axis_size("dp"), 0)]

    def step(self, token=None):
        mask = self.todo.pop(0)
        experts, tok = self.logits.shape
        if mask[1]:
            wide = jnp.pad(self.logits, ((0, 0), (0, self.routers.shape[1] - tok)))
            mine = jnp.concatenate([wide, self.routers], axis=0)
        else:
            if self.whole is None:
                whole = jnp.concatenate([self.logits, self.rest], axis=0)
                self.whole = jnp.pad(whole, ((0, -whole.shape[0] % 8), (0, 0)))[None]
            mine = self.whole
        if token is not None:
            mine, _ = lax.optimization_barrier((mine, token))
        other = send(mine, mask)
        if mask[1]:
            self.logits = self.logits + other[:experts, :tok]
            self.routers = jnp.concatenate([self.routers, other[experts:]], axis=0)
        else:
            self.whole = jnp.concatenate([mine, other], axis=0)

    def finish(self):
        while self.todo:
            self.step()
        return self.whole, self.routers.reshape(-1, self.logits.shape[0], self.routers.shape[1])


def route_g_kernel(sizes, my_ref, pid_ref, *refs):
    dps, cap, pblk, seqs, suf = sizes
    pieces, routing = refs[:8], refs[8]
    out, away, sums = refs[-3:]
    features = sums.shape[-1]
    sums[...] = jnp.zeros_like(sums)
    for md in range(dps):
        group = my_ref[0] ^ md
        for s in range(seqs):
            block = pid_ref[group * seqs + s]
            low = suf + s * pblk
            sums[block] += pieces[md % 8][0, 0, md // 8, low : low + pblk, :].astype(F32)
    for md in range(dps):
        group = my_ref[0] ^ md
        prefix = sums[pl.ds(group * PREF_DP, PREF_DP)].reshape(PREF_DP * pblk, features)
        cot = jnp.concatenate([prefix.astype(BF16), pieces[md % 8][0, 0, md // 8, :suf]], axis=0)
        both = jnp.dot(routing[group], cot, preferred_element_type=F32).astype(BF16)
        out[group] = both[:cap]
        away[group] = both[cap:]


def route_x_kernel(sizes, my_ref, pid_ref, *refs):
    dps, cap = sizes[:2]
    pieces, routing = refs[:8], refs[8]
    out, away = refs[-2:]
    for md in range(dps):
        group = my_ref[0] ^ md
        both = jnp.dot(routing[group], pieces[md % 8][0, 0, md // 8], preferred_element_type=F32).astype(BF16)
        out[group] = both[:cap]
        away[group] = both[cap:]


def route(pieces, y, k, my_dp, my_e, prefix_ids, routing, prior, sizes):
    dps, twice_cap, tok = routing.shape
    cap = twice_cap // 2
    eights = [pieces[md, y] for md in range(8)]
    _, _, ex_dp, rows, features = eights[0][0].shape
    n_e = lax.axis_size("expert")
    scalars = jnp.stack([my_dp, my_e ^ (2 * y + 4 * k)]).astype(jnp.int32)
    block = pl.BlockSpec((dps, cap, features), lambda i, my, pid: (0, 0, my[1]))
    in_specs = [
        pl.BlockSpec((1, 1, ex_dp, rows, features), lambda i, my, pid, at=at: (at, k, 0, 0, 0))
        for _, at in eights
    ]
    in_specs += [pl.BlockSpec((dps, twice_cap, tok), lambda i, my, pid: (0, 0, 0))]
    operands = [*(piece for piece, _ in eights), routing]
    aliases = {}
    if prior is not None:
        in_specs += [pl.BlockSpec(memory_space=pl.ANY)]
        aliases = {2 + len(operands): 0}
        operands += [prior]
    scratch, kernel, name = [], route_x_kernel, "route_x"
    if sizes is not None:
        scratch = [pltpu.VMEM((dps * PREF_DP, sizes[0], features), F32)]
        kernel, name = route_g_kernel, "route_g"
    return pl.pallas_call(
        functools.partial(kernel, (dps, cap, *(sizes or ()))),
        out_shape=(
            jax.ShapeDtypeStruct((dps, cap, n_e * features), BF16),
            jax.ShapeDtypeStruct((dps, cap, features), BF16),
        ),
        grid_spec=pltpu.PrefetchScalarGridSpec(
            num_scalar_prefetch=2,
            grid=(1,),
            in_specs=in_specs,
            out_specs=(block, pl.BlockSpec((dps, cap, features), lambda i, my, pid: (0, 0, 0))),
            scratch_shapes=scratch,
        ),
        input_output_aliases=aliases,
        compiler_params=pltpu.CompilerParams(vmem_limit_bytes=56 * MIB),
        cost_estimate=pl.CostEstimate(flops=4 * GFLOP // 2, bytes_accessed=16 * MIB, transcendentals=0),
        name=name,
    )(scalars, prefix_ids, *operands)


def routed_rows(pieces, my_dp, my_e, prefix_ids, routing, sizes):
    whole, away = None, []
    n_e, features = lax.axis_size("expert"), pieces[0, 0][0].shape[-1]
    for k in range(n_e // 4):
        for y in range(2):
            whole, part = route(pieces, y, k, my_dp, my_e, prefix_ids, routing, whole, sizes)
            away.append((2 * y + 4 * k, send(part, C)))
    for me, part in away:
        whole = lax.dynamic_update_slice(whole, part, (0, 0, (my_e ^ me ^ 1) * features))
    return whole.reshape(-1, n_e * features)


def dx_kernel(my_ref, da, db, dl, gate_w, up_w, router, tokens_of, out):
    nt = (((1,), (1,)), ((), ()))
    total = lax.dot_general(da[...], gate_w[...], nt, preferred_element_type=F32)
    total = total + lax.dot_general(db[...], up_w[...], nt, preferred_element_type=F32)
    total = total + jnp.dot(dl[...], router[0], preferred_element_type=F32)
    fours, tok, cap = tokens_of.shape
    for four in range(fours):
        place = (my_ref[1] // 4) ^ four
        rows = total[four * cap : (four + 1) * cap].astype(BF16)
        by_token = jnp.dot(tokens_of[place], rows, preferred_element_type=F32)
        out[0, pl.ds(pl.multiple_of(place * tok, tok), tok)] = by_token.astype(BF16)


def dx_tokens(d_a, d_b, dl, gate_w, up_w, routers, tokens_of, my_dp, my_e, top):
    rows, hidden = d_a.shape
    features = routers.shape[2]
    all_tok = tokens_of.shape[0] * tokens_of.shape[1]
    cuts = 2 if features % 256 == 0 else 1
    wide = features // cuts
    full = lambda *shape: pl.BlockSpec(shape, lambda i, j, my: (0,) * len(shape))
    weight = pl.BlockSpec((wide, hidden), lambda i, j, my: ((my[0] ^ (top - i)) * cuts + j, 0))
    return pl.pallas_call(
        dx_kernel,
        out_shape=jax.ShapeDtypeStruct((2, all_tok, features), BF16),
        grid_spec=pltpu.PrefetchScalarGridSpec(
            num_scalar_prefetch=1,
            grid=(2, cuts),
            in_specs=[
                full(rows, hidden),
                full(rows, hidden),
                full(*dl.shape),
                weight,
                weight,
                pl.BlockSpec((1, routers.shape[1], wide), lambda i, j, my: (top - i, 0, j)),
                full(*tokens_of.shape),
            ],
            out_specs=pl.BlockSpec((1, all_tok, wide), lambda i, j, my: (i, 0, j)),
        ),
        compiler_params=pltpu.CompilerParams(vmem_limit_bytes=56 * MIB),
        cost_estimate=pl.CostEstimate(flops=12 * GFLOP, bytes_accessed=12 * MIB, transcendentals=0),
        name="dx",
    )(jnp.stack([my_e, my_dp]).astype(jnp.int32), d_a, d_b, dl, gate_w, up_w, routers, tokens_of)


def add(*terms):
    total = terms[0].astype(F32)
    for term in terms[1:]:
        total = total + term.astype(F32)
    return total.astype(BF16)


def reduce_tokens(parts):
    n_e, n_dp = lax.axis_size("expert"), lax.axis_size("dp")
    for bit in reversed(bits(n_e, 2)):
        for me in range(bit):
            parts[me] = add(parts[me], send(parts.pop(me + bit), (0, bit)))
    for bit in reversed(bits(n_dp, 3)):
        for me in parts:
            parts[me] = add(parts[me][:bit], send(parts[me][bit:], (bit, 0)))
    _, tok, features = parts[0].shape
    half = tok // 2
    near, far = {}, {}
    for me in (2, 0):
        mine = parts[me].reshape(4, 2, tok, features)
        other = send(parts[me + 1], C).reshape(4, 2, tok, features)
        for x in range(2):
            near[me, x] = add(mine[:, x, :half], other[:, x, :half])
            if me == 0:
                far[me, x] = add(mine[:, x, half:], other[:, x, half:])
        if me == 2:
            far_y = add(mine[:, :, half:], other[:, :, half:])
    from_y = send(far_y, Y)
    near_y = add(near[2, 0], send(near[2, 1], X))
    far_1 = add(far[0, 1], from_y[:, 1])
    far_0 = add(far[0, 0], from_y[:, 0])
    near_0 = add(near[0, 0], send(near[0, 1], X))
    a = add(near_0, send(near_y, Y))
    b = add(far_0, send(far_1, X))
    both = [jnp.concatenate([a[z], b[z]], axis=0) for z in range(4)]
    both[2] = add(both[2], send(both[3], Z1))
    return add(both[0], send(both[2], Z2), send(both[1], Z1))


def body(
    tokens,
    suffix_cotangent,
    prefix_partials,
    prefix_of_seq,
    expert_ids,
    router_weight,
    gate_weight,
    up_weight,
    down_weight,
    gate_pre,
    up_pre,
):
    n_dp, n_e = lax.axis_size("dp"), lax.axis_size("expert")
    my_dp, my_e = lax.axis_index("dp"), lax.axis_index("expert")
    tok, features = tokens.shape
    seqs, pblk, _ = prefix_partials.shape
    suf = suffix_cotangent.shape[0]
    experts = router_weight.shape[1]
    row_total, hidden_here = gate_pre.shape[1:]
    cap = row_total // n_dp

    raw = jnp.concatenate([suffix_cotangent, prefix_partials.reshape(seqs * pblk, features)], axis=0)
    router_t = router_weight.T
    logits_here = lax.dot_general(router_t, tokens, (((1,), (1,)), ((), ())), preferred_element_type=F32)
    seq_row = jnp.pad(prefix_of_seq.astype(F32)[None], ((0, 0), (0, tok - seqs)))
    rest = jnp.concatenate([expert_ids.T.astype(F32), seq_row], axis=0)
    small = SmallGather(logits_here, router_t.astype(F32), rest)
    small.step()
    pieces = gather_tree(raw)
    for mask in SMALL_AT:
        small.step(pieces[mask])
    column = gather_column(tokens, pieces[X_AT])
    small, routers = small.finish()

    small = jnp.take(small, my_dp ^ jnp.arange(n_dp, dtype=jnp.int32), axis=0)
    logits = small[:, :experts]
    ids = small[:, experts : experts + 2].astype(jnp.int32)
    prefix_ids = small[:, experts + 2, :seqs].astype(jnp.int32).reshape(-1)
    first, second = ids[:, 0], ids[:, 1]
    iota_e = jnp.arange(experts, dtype=jnp.int32)[None, :, None]
    is_first = (first[:, None] == iota_e).astype(F32)
    is_second = (second[:, None] == iota_e).astype(F32)
    first_prob = jax.nn.sigmoid(jnp.sum(logits * (is_first - is_second), axis=1))
    second_prob = 1.0 - first_prob
    earlier = jnp.triu(jnp.ones((tok, tok), F32), 1)
    slots = jnp.arange(cap, dtype=jnp.int32)[None, :, None]

    def placing(expert):
        mine = (first == expert) | (second == expert)
        slot = jnp.dot(mine.astype(F32), earlier).astype(jnp.int32)
        slot = jnp.where(mine, slot, -1)
        return slot, slot[:, None, :] == slots

    slot, placed = placing(my_e)
    _, placed_other = placing(my_e ^ 1)
    routing = jnp.concatenate([placed, placed_other], axis=1).astype(BF16)
    relative = my_dp ^ jnp.arange(n_dp, dtype=jnp.int32)
    row_of = jnp.where(slot < 0, -1, slot + cap * (jnp.arange(n_dp, dtype=jnp.int32) % 4)[:, None])
    row_of = jnp.take(row_of, relative, axis=0).reshape(-1, 4 * tok, 1)
    tokens_of = (row_of == jnp.arange(4 * cap, dtype=jnp.int32)[None, None]).astype(BF16)
    prob_here = jnp.where(first == my_e, first_prob, second_prob)
    weight_col = (
        jnp.sum(jnp.where(placed, prob_here[:, None, :], 0.0), axis=2)
        .astype(BF16)
        .astype(F32)
        .reshape(row_total, 1)
    )
    other = jnp.where(first == my_e, second, first)
    product = first_prob * second_prob
    router_col = jnp.stack(
        [
            jnp.sum(
                jnp.where(
                    placed,
                    (
                        product
                        * ((my_e == e).astype(F32) - (other == e).astype(F32))
                    )[:, None, :],
                    0.0,
                ),
                axis=2,
            ).reshape(row_total)
            for e in range(experts)
        ],
        axis=1,
    )

    g_pieces = {(md, y): (pieces[md, 2 * y][None], 0) for md in range(8) for y in range(2)}
    rows_g = routed_rows(g_pieces, my_dp, my_e, prefix_ids, routing, (pblk, seqs, suf))
    over_x, over_y = send(column, X), send(column, Y)

    gate_w, up_w, down_w = gate_weight[0], up_weight[0], down_weight[0]
    gate_act = gate_pre[0].astype(F32)
    up_act = up_pre[0].astype(F32)
    sigmoid_a = jax.nn.sigmoid(gate_act)
    activation = gate_act * sigmoid_a
    slope = sigmoid_a * (1.0 + gate_act * (1.0 - sigmoid_a))
    hidden = activation * up_act
    d_hidden = lax.dot_general(
        rows_g, down_w, (((1,), (1,)), ((), ())), preferred_element_type=F32
    )
    dots = jnp.sum(hidden * d_hidden, axis=1)
    scaled = weight_col * d_hidden
    weighted = (weight_col * hidden).astype(BF16)
    d_a = (scaled * up_act * slope).astype(BF16)
    d_b = (scaled * activation).astype(BF16)

    d_a, d_b, over_x, over_y = lax.optimization_barrier((d_a, d_b, over_x, over_y))
    corner = send(over_y[:2], X), send(over_x[2:], Y)
    dl = dots[:, None] * router_col
    dl_high = dl.astype(BF16)
    dl_low = (dl - dl_high.astype(F32)).astype(BF16)
    dl = jnp.concatenate([dl_high, dl_low], axis=1)
    routers = jnp.concatenate([routers, routers], axis=1).astype(BF16)
    parts = {}
    for top in range(n_e - 1, 0, -2):
        if top == 1:
            d_a, d_b, corner = lax.optimization_barrier((d_a, d_b, corner))
        pair = dx_tokens(d_a, d_b, dl, gate_w, up_w, routers, tokens_of, my_dp, my_e, top)
        for i in range(2):
            parts[top - i] = pair[i].reshape(n_dp, tok, features)
    x_pieces = {}
    for z in range(4):
        x_pieces[2 * z, 0], x_pieces[2 * z + 1, 0] = (column, z), (over_x, z)
        x_pieces[2 * z, 1], x_pieces[2 * z + 1, 1] = (over_y, z), (corner[z // 2], z % 2)
    rows_x = routed_rows(x_pieces, my_dp, my_e, prefix_ids, routing, None)
    d_tokens = reduce_tokens(parts)

    tn = (((0,), (0,)), ((), ()))
    grad_down = lax.dot_general(weighted, rows_g, tn, preferred_element_type=F32)
    grad_gate = lax.dot_general(rows_x, d_a, tn, preferred_element_type=F32)
    grad_up = lax.dot_general(rows_x, d_b, tn, preferred_element_type=F32)
    return (
        d_tokens,
        grad_gate.astype(BF16)[None],
        grad_up.astype(BF16)[None],
        grad_down.astype(BF16)[None],
    )


def solution(mesh):
    return jax.shard_map(
        body,
        mesh=mesh,
        in_specs=(
            P("dp", "expert"),
            P("dp", "expert"),
            P("dp", None, "expert"),
            P("dp"),
            P("dp", None),
            P("expert", None),
            P("expert", None, "dp"),
            P("expert", None, "dp"),
            P("expert", "dp", None),
            P("expert", None, "dp"),
            P("expert", None, "dp"),
        ),
        out_specs=(
            P("dp", "expert"),
            P("expert", None, "dp"),
            P("expert", None, "dp"),
            P("expert", "dp", None),
        ),
        check_vma=False,
    )
```

```python
import functools

import jax
import jax.numpy as jnp
from jax import lax
from jax.experimental import pallas as pl
from jax.experimental.pallas import tpu as pltpu
from jax.sharding import PartitionSpec as P

PREF_DP = 2
AXES = ("dp", "expert")
F32, BF16 = jnp.float32, jnp.bfloat16
MIB = 1 << 20
GFLOP = 10**9
X, Z1, Z2, Y, C = (1, 0), (2, 0), (4, 0), (0, 2), (0, 1)


def xor(a, b):
    return a[0] ^ b[0], a[1] ^ b[1]


def send(value, mask):
    dps, experts = lax.axis_size("dp"), lax.axis_size("expert")
    pairs = [
        (d * experts + e, (d ^ mask[0]) * experts + (e ^ mask[1]))
        for d in range(dps)
        for e in range(experts)
    ]
    return lax.ppermute(value, AXES, pairs)


def bits(count, start):
    return [1 << b for b in range(start, count.bit_length() - 1)]


TREE = [
    (Z2, (0, 0)),
    (X, (0, 0)),
    (Y, (0, 0)),
    (Z1, (0, 0)),
    (Y, (1, 0)),
    (Z1, (0, 2)),
    (X, (4, 0)),
    (Y, (4, 0)),
    (Z1, (4, 0)),
    (X, (2, 0)),
    (Y, (5, 0)),
    (Z1, (4, 2)),
    (X, (6, 0)),
    (Y, (3, 0)),
    (Z1, (5, 2)),
]
X_AT = (5, 0)
SMALL_AT = ((2, 0), (4, 0), (6, 0), (6, 2))


def whole_extra(rows):
    base = rows[None, None]
    for bit in bits(lax.axis_size("dp"), 3):
        base = jnp.concatenate([base, send(base, (bit, 0))], axis=1)
    for bit in bits(lax.axis_size("expert"), 2):
        base = jnp.concatenate([base, send(base, (0, bit))], axis=0)
    return base


def gather_tree(rows):
    pieces = {(0, 0): whole_extra(rows)}
    for link, mask in TREE:
        pieces[xor(link, mask)] = send(pieces[mask], link)
    return pieces


def gather_column(rows, token):
    base, _ = lax.optimization_barrier((whole_extra(rows), token))
    two, one = send(base, Z2), send(base, Z1)
    return jnp.stack([base, one, two, send(two, Z1)])


class SmallGather:
    def __init__(self, logits, router_t, rest):
        self.logits, self.routers, self.rest, self.whole = logits, router_t, rest, None
        self.todo = [(0, bit) for bit in bits(lax.axis_size("expert"), 0)]
        self.todo += [(bit, 0) for bit in bits(lax.axis_size("dp"), 0)]

    def step(self, token=None):
        mask = self.todo.pop(0)
        experts, tok = self.logits.shape
        if mask[1]:
            wide = jnp.pad(self.logits, ((0, 0), (0, self.routers.shape[1] - tok)))
            mine = jnp.concatenate([wide, self.routers], axis=0)
        else:
            if self.whole is None:
                whole = jnp.concatenate([self.logits, self.rest], axis=0)
                self.whole = jnp.pad(whole, ((0, -whole.shape[0] % 8), (0, 0)))[None]
            mine = self.whole
        if token is not None:
            mine, _ = lax.optimization_barrier((mine, token))
        other = send(mine, mask)
        if mask[1]:
            self.logits = self.logits + other[:experts, :tok]
            self.routers = jnp.concatenate([self.routers, other[experts:]], axis=0)
        else:
            self.whole = jnp.concatenate([mine, other], axis=0)

    def finish(self):
        while self.todo:
            self.step()
        return self.whole, self.routers.reshape(-1, self.logits.shape[0], self.routers.shape[1])


def route_g_kernel(sizes, my_ref, pid_ref, *refs):
    dps, cap, pblk, seqs, suf = sizes
    pieces, routing = refs[:8], refs[8]
    out, away, sums = refs[-3:]
    features = sums.shape[-1]
    sums[...] = jnp.zeros_like(sums)
    for md in range(dps):
        group = my_ref[0] ^ md
        for s in range(seqs):
            block = pid_ref[group * seqs + s]
            low = suf + s * pblk
            sums[block] += pieces[md % 8][0, 0, md // 8, low : low + pblk, :].astype(F32)
    for md in range(dps):
        group = my_ref[0] ^ md
        prefix = sums[pl.ds(group * PREF_DP, PREF_DP)].reshape(PREF_DP * pblk, features)
        cot = jnp.concatenate([prefix.astype(BF16), pieces[md % 8][0, 0, md // 8, :suf]], axis=0)
        both = jnp.dot(routing[group], cot, preferred_element_type=F32).astype(BF16)
        out[group] = both[:cap]
        away[group] = both[cap:]


def route_x_kernel(sizes, my_ref, pid_ref, *refs):
    dps, cap = sizes[:2]
    pieces, routing = refs[:8], refs[8]
    out, away = refs[-2:]
    for md in range(dps):
        group = my_ref[0] ^ md
        both = jnp.dot(routing[group], pieces[md % 8][0, 0, md // 8], preferred_element_type=F32).astype(BF16)
        out[group] = both[:cap]
        away[group] = both[cap:]


def route(pieces, y, k, my_dp, my_e, prefix_ids, routing, prior, sizes):
    dps, twice_cap, tok = routing.shape
    cap = twice_cap // 2
    eights = [pieces[md, y] for md in range(8)]
    _, _, ex_dp, rows, features = eights[0][0].shape
    n_e = lax.axis_size("expert")
    scalars = jnp.stack([my_dp, my_e ^ (2 * y + 4 * k)]).astype(jnp.int32)
    block = pl.BlockSpec((dps, cap, features), lambda i, my, pid: (0, 0, my[1]))
    in_specs = [
        pl.BlockSpec((1, 1, ex_dp, rows, features), lambda i, my, pid, at=at: (at, k, 0, 0, 0))
        for _, at in eights
    ]
    in_specs += [pl.BlockSpec((dps, twice_cap, tok), lambda i, my, pid: (0, 0, 0))]
    operands = [*(piece for piece, _ in eights), routing]
    aliases = {}
    if prior is not None:
        in_specs += [pl.BlockSpec(memory_space=pl.ANY)]
        aliases = {2 + len(operands): 0}
        operands += [prior]
    scratch, kernel, name = [], route_x_kernel, "route_x"
    if sizes is not None:
        scratch = [pltpu.VMEM((dps * PREF_DP, sizes[0], features), F32)]
        kernel, name = route_g_kernel, "route_g"
    return pl.pallas_call(
        functools.partial(kernel, (dps, cap, *(sizes or ()))),
        out_shape=(
            jax.ShapeDtypeStruct((dps, cap, n_e * features), BF16),
            jax.ShapeDtypeStruct((dps, cap, features), BF16),
        ),
        grid_spec=pltpu.PrefetchScalarGridSpec(
            num_scalar_prefetch=2,
            grid=(1,),
            in_specs=in_specs,
            out_specs=(block, pl.BlockSpec((dps, cap, features), lambda i, my, pid: (0, 0, 0))),
            scratch_shapes=scratch,
        ),
        input_output_aliases=aliases,
        compiler_params=pltpu.CompilerParams(
            vmem_limit_bytes=(16 if dps <= 8 and sizes is None else 56) * MIB
        ),
        cost_estimate=pl.CostEstimate(flops=4 * GFLOP // 2, bytes_accessed=16 * MIB, transcendentals=0),
        name=name,
    )(scalars, prefix_ids, *operands)


def routed_rows(pieces, my_dp, my_e, prefix_ids, routing, sizes):
    whole, away = None, []
    n_e, features = lax.axis_size("expert"), pieces[0, 0][0].shape[-1]
    for k in range(n_e // 4):
        for y in range(2):
            whole, part = route(pieces, y, k, my_dp, my_e, prefix_ids, routing, whole, sizes)
            away.append((2 * y + 4 * k, send(part, C)))
    for me, part in away:
        whole = lax.dynamic_update_slice(whole, part, (0, 0, (my_e ^ me ^ 1) * features))
    return whole.reshape(-1, n_e * features)


def dx_kernel(my_ref, da, db, dl, gate_w, up_w, router, tokens_of, out):
    nt = (((1,), (1,)), ((), ()))
    total = lax.dot_general(da[...], gate_w[...], nt, preferred_element_type=F32)
    total = total + lax.dot_general(db[...], up_w[...], nt, preferred_element_type=F32)
    total = total + jnp.dot(dl[...], router[0], preferred_element_type=F32)
    fours, tok, cap = tokens_of.shape
    for four in range(fours):
        place = (my_ref[1] // 4) ^ four
        rows = total[four * cap : (four + 1) * cap].astype(BF16)
        by_token = jnp.dot(tokens_of[place], rows, preferred_element_type=F32)
        out[0, pl.ds(pl.multiple_of(place * tok, tok), tok)] = by_token.astype(BF16)


def dx_tokens(d_a, d_b, dl, gate_w, up_w, routers, tokens_of, my_dp, my_e, top):
    rows, hidden = d_a.shape
    features = routers.shape[2]
    all_tok = tokens_of.shape[0] * tokens_of.shape[1]
    cuts = 2 if features % 256 == 0 else 1
    wide = features // cuts
    full = lambda *shape: pl.BlockSpec(shape, lambda i, j, my: (0,) * len(shape))
    weight = pl.BlockSpec((wide, hidden), lambda i, j, my: ((my[0] ^ (top - i)) * cuts + j, 0))
    return pl.pallas_call(
        dx_kernel,
        out_shape=jax.ShapeDtypeStruct((2, all_tok, features), BF16),
        grid_spec=pltpu.PrefetchScalarGridSpec(
            num_scalar_prefetch=1,
            grid=(2, cuts),
            in_specs=[
                full(rows, hidden),
                full(rows, hidden),
                full(*dl.shape),
                weight,
                weight,
                pl.BlockSpec((1, routers.shape[1], wide), lambda i, j, my: (top - i, 0, j)),
                full(*tokens_of.shape),
            ],
            out_specs=pl.BlockSpec((1, all_tok, wide), lambda i, j, my: (i, 0, j)),
        ),
        compiler_params=pltpu.CompilerParams(vmem_limit_bytes=56 * MIB),
        cost_estimate=pl.CostEstimate(flops=12 * GFLOP, bytes_accessed=12 * MIB, transcendentals=0),
        name="dx",
    )(jnp.stack([my_e, my_dp]).astype(jnp.int32), d_a, d_b, dl, gate_w, up_w, routers, tokens_of)


def add(*terms):
    total = terms[0].astype(F32)
    for term in terms[1:]:
        total = total + term.astype(F32)
    return total.astype(BF16)


def reduce_tokens(parts):
    n_e, n_dp = lax.axis_size("expert"), lax.axis_size("dp")
    for bit in reversed(bits(n_e, 2)):
        for me in range(bit):
            parts[me] = add(parts[me], send(parts.pop(me + bit), (0, bit)))
    for bit in reversed(bits(n_dp, 3)):
        for me in parts:
            parts[me] = add(parts[me][:bit], send(parts[me][bit:], (bit, 0)))
    _, tok, features = parts[0].shape
    half = tok // 2
    near, far = {}, {}
    for me in (2, 0):
        mine = parts[me].reshape(4, 2, tok, features)
        other = send(parts[me + 1], C).reshape(4, 2, tok, features)
        for x in range(2):
            near[me, x] = add(mine[:, x, :half], other[:, x, :half])
            if me == 0:
                far[me, x] = add(mine[:, x, half:], other[:, x, half:])
        if me == 2:
            far_y = add(mine[:, :, half:], other[:, :, half:])
    from_y = send(far_y, Y)
    near_y = add(near[2, 0], send(near[2, 1], X))
    far_1 = add(far[0, 1], from_y[:, 1])
    far_0 = add(far[0, 0], from_y[:, 0])
    near_0 = add(near[0, 0], send(near[0, 1], X))
    a = add(near_0, send(near_y, Y))
    b = add(far_0, send(far_1, X))
    both = [jnp.concatenate([a[z], b[z]], axis=0) for z in range(4)]
    both[2] = add(both[2], send(both[3], Z1))
    return add(both[0], send(both[2], Z2), send(both[1], Z1))


def body(
    tokens,
    suffix_cotangent,
    prefix_partials,
    prefix_of_seq,
    expert_ids,
    router_weight,
    gate_weight,
    up_weight,
    down_weight,
    gate_pre,
    up_pre,
):
    n_dp, n_e = lax.axis_size("dp"), lax.axis_size("expert")
    my_dp, my_e = lax.axis_index("dp"), lax.axis_index("expert")
    tok, features = tokens.shape
    seqs, pblk, _ = prefix_partials.shape
    suf = suffix_cotangent.shape[0]
    experts = router_weight.shape[1]
    row_total, hidden_here = gate_pre.shape[1:]
    cap = row_total // n_dp

    raw = jnp.concatenate([suffix_cotangent, prefix_partials.reshape(seqs * pblk, features)], axis=0)
    router_t = router_weight.T
    logits_here = lax.dot_general(router_t, tokens, (((1,), (1,)), ((), ())), preferred_element_type=F32)
    seq_row = jnp.pad(prefix_of_seq.astype(F32)[None], ((0, 0), (0, tok - seqs)))
    rest = jnp.concatenate([expert_ids.T.astype(F32), seq_row], axis=0)
    small = SmallGather(logits_here, router_t.astype(F32), rest)
    small.step()
    pieces = gather_tree(raw)
    for mask in SMALL_AT:
        small.step(pieces[mask])
    column = gather_column(tokens, pieces[X_AT])
    small, routers = small.finish()

    small = jnp.take(small, my_dp ^ jnp.arange(n_dp, dtype=jnp.int32), axis=0)
    logits = small[:, :experts]
    ids = small[:, experts : experts + 2].astype(jnp.int32)
    prefix_ids = small[:, experts + 2, :seqs].astype(jnp.int32).reshape(-1)
    first, second = ids[:, 0], ids[:, 1]
    iota_e = jnp.arange(experts, dtype=jnp.int32)[None, :, None]
    is_first = (first[:, None] == iota_e).astype(F32)
    is_second = (second[:, None] == iota_e).astype(F32)
    first_prob = jax.nn.sigmoid(jnp.sum(logits * (is_first - is_second), axis=1))
    second_prob = 1.0 - first_prob
    earlier = jnp.triu(jnp.ones((tok, tok), F32), 1)
    slots = jnp.arange(cap, dtype=jnp.int32)[None, :, None]

    def placing(expert):
        mine = (first == expert) | (second == expert)
        slot = jnp.dot(mine.astype(F32), earlier).astype(jnp.int32)
        slot = jnp.where(mine, slot, -1)
        return slot, slot[:, None, :] == slots

    slot, placed = placing(my_e)
    _, placed_other = placing(my_e ^ 1)
    routing = jnp.concatenate([placed, placed_other], axis=1).astype(BF16)
    relative = my_dp ^ jnp.arange(n_dp, dtype=jnp.int32)
    row_of = jnp.where(slot < 0, -1, slot + cap * (jnp.arange(n_dp, dtype=jnp.int32) % 4)[:, None])
    row_of = jnp.take(row_of, relative, axis=0).reshape(-1, 4 * tok, 1)
    tokens_of = (row_of == jnp.arange(4 * cap, dtype=jnp.int32)[None, None]).astype(BF16)
    prob_here = jnp.where(first == my_e, first_prob, second_prob)
    weight_col = (
        jnp.sum(jnp.where(placed, prob_here[:, None, :], 0.0), axis=2)
        .astype(BF16)
        .astype(F32)
        .reshape(row_total, 1)
    )
    other = jnp.where(first == my_e, second, first)
    product = first_prob * second_prob
    router_col = jnp.stack(
        [
            jnp.sum(
                jnp.where(
                    placed,
                    (
                        product
                        * ((my_e == e).astype(F32) - (other == e).astype(F32))
                    )[:, None, :],
                    0.0,
                ),
                axis=2,
            ).reshape(row_total)
            for e in range(experts)
        ],
        axis=1,
    )

    g_pieces = {(md, y): (pieces[md, 2 * y][None], 0) for md in range(8) for y in range(2)}
    rows_g = routed_rows(g_pieces, my_dp, my_e, prefix_ids, routing, (pblk, seqs, suf))
    over_x, over_y = send(column, X), send(column, Y)

    gate_w, up_w, down_w = gate_weight[0], up_weight[0], down_weight[0]
    gate_act = gate_pre[0].astype(F32)
    up_act = up_pre[0].astype(F32)
    sigmoid_a = jax.nn.sigmoid(gate_act)
    activation = gate_act * sigmoid_a
    slope = sigmoid_a * (1.0 + gate_act * (1.0 - sigmoid_a))
    hidden = activation * up_act
    d_hidden = lax.dot_general(
        rows_g, down_w, (((1,), (1,)), ((), ())), preferred_element_type=F32
    )
    dots = jnp.sum(hidden * d_hidden, axis=1)
    scaled = weight_col * d_hidden
    weighted = (weight_col * hidden).astype(BF16)
    d_a = (scaled * up_act * slope).astype(BF16)
    d_b = (scaled * activation).astype(BF16)

    d_a, d_b, over_x, over_y = lax.optimization_barrier((d_a, d_b, over_x, over_y))
    corner = send(over_y[:2], X), send(over_x[2:], Y)
    dl = dots[:, None] * router_col
    dl_high = dl.astype(BF16)
    dl_low = (dl - dl_high.astype(F32)).astype(BF16)
    dl = jnp.concatenate([dl_high, dl_low], axis=1)
    routers = jnp.concatenate([routers, routers], axis=1).astype(BF16)
    parts = {}
    for top in range(n_e - 1, 0, -2):
        if top == 1:
            d_a, d_b, corner = lax.optimization_barrier((d_a, d_b, corner))
        pair = dx_tokens(d_a, d_b, dl, gate_w, up_w, routers, tokens_of, my_dp, my_e, top)
        for i in range(2):
            parts[top - i] = pair[i].reshape(n_dp, tok, features)
    x_pieces = {}
    for z in range(4):
        x_pieces[2 * z, 0], x_pieces[2 * z + 1, 0] = (column, z), (over_x, z)
        x_pieces[2 * z, 1], x_pieces[2 * z + 1, 1] = (over_y, z), (corner[z // 2], z % 2)
    rows_x = routed_rows(x_pieces, my_dp, my_e, prefix_ids, routing, None)
    d_tokens = reduce_tokens(parts)

    tn = (((0,), (0,)), ((), ()))
    grad_down = lax.dot_general(weighted, rows_g, tn, preferred_element_type=F32)
    grad_gate = lax.dot_general(rows_x, d_a, tn, preferred_element_type=F32)
    grad_up = lax.dot_general(rows_x, d_b, tn, preferred_element_type=F32)
    return (
        d_tokens,
        grad_gate.astype(BF16)[None],
        grad_up.astype(BF16)[None],
        grad_down.astype(BF16)[None],
    )


def solution(mesh):
    return jax.shard_map(
        body,
        mesh=mesh,
        in_specs=(
            P("dp", "expert"),
            P("dp", "expert"),
            P("dp", None, "expert"),
            P("dp"),
            P("dp", None),
            P("expert", None),
            P("expert", None, "dp"),
            P("expert", None, "dp"),
            P("expert", "dp", None),
            P("expert", None, "dp"),
            P("expert", None, "dp"),
        ),
        out_specs=(
            P("dp", "expert"),
            P("expert", None, "dp"),
            P("expert", None, "dp"),
            P("expert", "dp", None),
        ),
        check_vma=False,
    )
```
